256 devices in a mesh: ha: 16 (over z_hi, y), wa: 8 (over x, core), col: 2 (over z_lo).
Axes of the slice: x: 4, y: 4, z: 8 (z_hi: 4, z_lo: 2; z = z_hi * 2 + z_lo), core: 2. Of those that a mesh axis runs over, the one named last changes fastest.
Arguments:
- features: bfloat16 [2, 4, 64, 256, 96], P('col', None, 'ha', 'wa'), may hold values from -6 to 6
- gain_first: float32 [96], replicated, may hold values from 0.1 to 1.9
- bias_first: float32 [96], replicated, may hold values from -3 to 3
- kernel_first: bfloat16 [3, 3, 3, 96, 96], replicated, may hold values from -0.125 to 0.125
- gain_second: float32 [96], replicated, may hold values from 0.1 to 1.9
- bias_second: float32 [96], replicated, may hold values from -3 to 3
- kernel_second: bfloat16 [3, 3, 3, 96, 96], replicated, may hold values from -0.125 to 0.125
- reward_map: bfloat16 [2, 4, 64, 256, 96], P('col', None, 'ha', 'wa'), may hold values from -6 to 6
- target_scores: float32 [2], replicated, may hold values from -5 to 5
Outputs:
- grad_input: float32 [2, 4, 64, 256, 96], P('col', None, 'ha', 'wa')
- weight_grad: float32 [2, 3, 3, 3, 96, 96], P(None, None, None, None, 'ha')
The draws below stay inside these ranges and needn't reach their ends.
All inputs are finite; a program needn't handle non-finite values.
Results may differ from the reference program's by a relative error of at most 0.0049.
Values may be sent and summed in bfloat16 or wider, within the bound.
No kernel may reach another device: no remote copies, remote signals or barrier semaphores. Data moves between devices by JAX's collectives and lax.ppermute only.
A program may use at most 64 MiB of HBM per device.

```python
import jax
import jax.numpy as jnp
from jax import lax

C = 96
FRAMES = 4
CANDS = 2
NH = 64
NW = 256


def draw_reward_map(key, part):
    key = jax.random.fold_in(key, 11)
    key_base = jax.random.fold_in(key, 0)
    shape = (CANDS, FRAMES, NH, NW, C)
    rise = 3.0 ** (jnp.arange(NH, dtype=jnp.float32) / max(NH - 1, 1))
    base = jax.random.normal(key_base, shape, jnp.float32)
    field = base * rise[:, None, None] * 0.5
    return jnp.clip(field, -6.0, 6.0).astype(jnp.bfloat16)


def block_levels(own_key, dims, cuts, smallest, top_value):
    level, own = 1.0, jax.random.fold_in(own_key, 6)
    for position, shards_of in cuts:
        draws = jnp.exp(jax.random.uniform(jax.random.fold_in(own, position), (shards_of,), jnp.float32, smallest / len(cuts), top_value / len(cuts)))
        level = level * jnp.repeat(draws, dims[position] // shards_of).reshape([-1 if axis == position else 1 for axis in range(len(dims))])
    return level


def bell_draw(rng, dims, deviation, reach, cuts=(), held_as=jnp.bfloat16):
    drawn = deviation * jax.random.normal(rng, dims, jnp.float32)
    if cuts:
        drawn = drawn * block_levels(rng, dims, cuts, -0.22, 0.18)
    return jnp.clip(drawn, -reach, reach).astype(held_as)


def setup_inputs(seed: int = 0) -> dict:
    splits = jax.random.split(jax.random.key(seed), 10)
    features = bell_draw(splits[0], (CANDS, FRAMES, NH, NW, C), 1.0, 6.0, ((0, 2), (2, 16), (3, 8)))
    gain_first = jnp.clip(1.0 + 0.18 * jax.random.normal(splits[1], (C,), jnp.float32), 0.1, 1.9)
    bias_first = bell_draw(splits[2], (C,), 0.5, 3.0, (), jnp.float32)
    kernel_first = bell_draw(splits[3], (3, 3, 3, C, C), (27 * C) ** -0.5, 0.125)
    gain_second = jnp.clip(1.0 + 0.18 * jax.random.normal(splits[4], (C,), jnp.float32), 0.1, 1.9)
    bias_second = bell_draw(splits[5], (C,), 0.5, 3.0, (), jnp.float32)
    kernel_second = bell_draw(splits[6], (3, 3, 3, C, C), (27 * C) ** -0.5, 0.125)
    reward_map = draw_reward_map(jax.random.fold_in(splits[9], 71), 0)
    target_scores = bell_draw(splits[8], (CANDS,), 1.5, 5.0, (), jnp.float32)
    return dict(features=features, gain_first=gain_first, bias_first=bias_first, kernel_first=kernel_first, gain_second=gain_second, bias_second=bias_second, kernel_second=kernel_second, reward_map=reward_map, target_scores=target_scores)


def activate(values, gain):
    scaled = lax.rsqrt(lax.optimization_barrier(jnp.mean(values * values, axis=-1, keepdims=True)) + 1e-06)
    return jax.nn.silu(values * scaled * gain)

def activate_back(values, gain, cotangent):
    _, pull = jax.vjp(lambda inner: activate(inner, gain), values)
    return pull(cotangent)[0]

def conv_forward(padded, kernel):
    frames, height, across, channels = padded.shape
    out_h = height - 2
    out_w = across - 2
    timed = jnp.concatenate([jnp.zeros((2, height, across, channels), padded.dtype), padded], 0)
    summed = jnp.zeros((frames * out_h * out_w, kernel.shape[-1]), jnp.float32)
    for step_t in range(3):
        for step_h in range(3):
            for step_w in range(3):
                window = timed[step_t:step_t + frames, step_h:step_h + out_h, step_w:step_w + out_w].reshape(-1, channels)
                summed = summed + jnp.dot(window, kernel[step_t, step_h, step_w], preferred_element_type=jnp.float32)
    return summed.reshape(frames, out_h, out_w, -1)

def conv_transpose(padded, kernel):
    frames, height, across, channels = padded.shape
    out_h = height - 2
    out_w = across - 2
    timed = jnp.concatenate([padded, jnp.zeros((2, height, across, channels), padded.dtype)], 0)
    summed = jnp.zeros((frames * out_h * out_w, kernel.shape[3]), jnp.float32)
    for step_t in range(3):
        for step_h in range(3):
            for step_w in range(3):
                window = timed[2 - step_t:2 - step_t + frames, 2 - step_h:2 - step_h + out_h, 2 - step_w:2 - step_w + out_w].reshape(-1, channels)
                summed = summed + lax.dot_general(window, kernel[step_t, step_h, step_w], (((1,), (1,)), ((), ())), preferred_element_type=jnp.float32)
    return summed.reshape(frames, out_h, out_w, -1)

def kernel_grad(padded, grad_out):
    frames, height, across, channels = padded.shape
    out_h = height - 2
    out_w = across - 2
    timed = jnp.concatenate([jnp.zeros((2, height, across, channels), padded.dtype), padded], 0)
    flat_out = grad_out.reshape(-1, grad_out.shape[-1])
    pieces = []
    for step_t in range(3):
        for step_h in range(3):
            for step_w in range(3):
                window = timed[step_t:step_t + frames, step_h:step_h + out_h, step_w:step_w + out_w].reshape(-1, channels)
                pieces.append(lax.dot_general(window, flat_out, (((0,), (0,)), ((), ())), preferred_element_type=jnp.float32))
    return jnp.stack(pieces).reshape(3, 3, 3, channels, flat_out.shape[-1])

def pad_frame(values):
    return jnp.pad(values, ((0, 0), (1, 1), (1, 1), (0, 0)))

def reference(features, gain_first, bias_first, kernel_first, gain_second, bias_second, kernel_second, reward_map, target_scores):
    norm_reward = jnp.sqrt(jnp.float32(FRAMES * NH * NW * C))
    stored = []
    rewards = []
    for which in range(CANDS):
        feats = features[which].astype(jnp.float32)
        first = activate(feats, gain_first).astype(jnp.bfloat16)
        hidden = conv_forward(pad_frame(first), kernel_first) + bias_first
        second = activate(hidden, gain_second).astype(jnp.bfloat16)
        output = feats + conv_forward(pad_frame(second), kernel_second) + bias_second
        rewards.append(jnp.sum(output * reward_map[which].astype(jnp.float32)) / norm_reward)
        stored.append((first, hidden, second))
    grads = []
    grad_one = jnp.zeros((3, 3, 3, C, C), jnp.float32)
    grad_two = jnp.zeros((3, 3, 3, C, C), jnp.float32)
    for which in range(CANDS):
        other = 1 - which
        prob = 1.0 / (1.0 + jnp.exp(rewards[other] - rewards[which]))
        target = 1.0 / (1.0 + jnp.exp(target_scores[other] - target_scores[which]))
        delta = prob - target
        first, hidden, second = stored[which]
        cot = delta * reward_map[which].astype(jnp.float32)
        cot_low = cot.astype(jnp.bfloat16)
        back_second = conv_transpose(pad_frame(cot_low), kernel_second)
        grad_two = grad_two + kernel_grad(pad_frame(second), cot_low)
        grad_hidden = activate_back(hidden, gain_second, back_second).astype(jnp.bfloat16)
        back_first = conv_transpose(pad_frame(grad_hidden), kernel_first)
        grad_one = grad_one + kernel_grad(pad_frame(first), grad_hidden)
        grads.append(cot + activate_back(features[which].astype(jnp.float32), gain_first, back_first))
    scale_weight = 1.0 / jnp.sqrt(jnp.float32(FRAMES * NH * NW))
    return (jnp.stack(grads), jnp.stack([grad_one, grad_two]) * scale_weight)
```

```python
import jax
import jax.numpy as jnp
from jax import lax
from jax.experimental import pallas as pl
from jax.experimental.pallas import tpu as pltpu
from jax.sharding import PartitionSpec as P

F32 = jnp.float32
BF16 = jnp.bfloat16
EPS = 1e-06
LANES = 128
PITCH = 48


def dot(a, b, dims):
    return lax.dot_general(a, b, (dims, ((), ())), preferred_element_type=F32)


def act_parts(values, gain, channels):
    scale = lax.rsqrt(jnp.sum(values * values, axis=-1, keepdims=True) * (1.0 / channels) + EPS)
    inner = values * scale * gain
    sig = 1.0 / (1.0 + jnp.exp(-inner))
    return scale, inner, sig


def act_back(values, parts, gain, cotangent, channels):
    scale, inner, sig = parts
    pulled = cotangent * (sig * (1.0 + inner * (1.0 - sig))) * gain
    along = jnp.sum(pulled * values, axis=-1, keepdims=True) * (1.0 / channels)
    return scale * pulled - values * (scale * scale * scale * along)


def block_kernel(
    edge,
    ext,
    feats_own,
    map_own,
    k_first,
    k_second,
    vectors,
    perm,
    grad,
    packed,
    wide,
    first3,
    map3,
    hid,
    back3,
    w1f,
    w1b,
    w2b,
    taps,
):
    channels = feats_own.shape[-1]
    frames, rows, across = feats_own.shape[:3]
    gain_first = vectors[0:1]
    bias_first = vectors[1:2]
    gain_second = vectors[2:3]
    bias_second = vectors[3:4]

    w1f[...] = jnp.zeros_like(w1f)
    w1b[...] = jnp.zeros_like(w1b)
    w2b[...] = jnp.zeros_like(w2b)
    for tap in range(27):
        pair, dj = divmod(tap, 3)
        one = k_first[tap]
        w1f[pair, LANES * dj : LANES * dj + channels, 0:channels] = one
        w1b[pair, 0:channels, LANES * (2 - dj) : LANES * (2 - dj) + channels] = one
        w2b[pair, 0:channels, LANES * (2 - dj) : LANES * (2 - dj) + channels] = k_second[tap]

    wide[...] = jnp.zeros_like(wide)
    halo_w = ext.shape[2]
    wide[:, :, 0:halo_w, 0:channels] = ext[0:frames].astype(F32)
    feats = wide[...]
    _, inner, sig = act_parts(feats, gain_first, channels)
    wide[...] = inner * sig
    first3[0:2] = jnp.zeros((2,) + first3.shape[1:], BF16)
    for dj in range(3):
        first3[2:6, :, :, LANES * dj : LANES * (dj + 1)] = wide[:, :, dj : dj + PITCH, :].astype(BF16)
    wide[:, :, 0:halo_w, 0:channels] = ext[frames : 2 * frames].astype(F32)
    map3[4:6] = jnp.zeros((2,) + map3.shape[1:], BF16)
    for dj in range(3):
        map3[0:4, :, :, LANES * dj : LANES * (dj + 1)] = wide[:, :, dj : dj + PITCH, :].astype(BF16)

    count = frames * (rows + 2) * PITCH
    hidden = jnp.zeros((count, LANES), F32)
    back = jnp.zeros((count, LANES), F32)
    for pair in range(9):
        dt, di = divmod(pair, 3)
        hidden = hidden + dot(
            first3[dt : dt + frames, di : di + rows + 2].reshape(count, 3 * LANES), w1f[pair], ((1,), (0,))
        )
    hidden = hidden + bias_first
    for pair in range(9):
        dt, di = divmod(pair, 3)
        back = back + dot(
            map3[2 - dt : 2 - dt + frames, 2 - di : 4 - di + rows].reshape(count, 3 * LANES),
            w2b[pair],
            ((1,), (1,)),
        )

    parts = act_parts(hidden, gain_second, channels)
    shape4 = (frames, rows + 2, PITCH, LANES)
    row = lax.broadcasted_iota(jnp.int32, shape4, 1)
    column = lax.broadcasted_iota(jnp.int32, shape4, 2)
    own = (column >= 1) & (column <= across)
    second = jnp.where(own, (parts[1] * parts[2]).reshape(shape4), 0.0)[:, 1 : rows + 1].astype(BF16)
    back4 = back.reshape(shape4)[:, 1 : rows + 1]
    own_f = feats_own[...].astype(F32)
    own_g = map_own[...].astype(F32)
    value = jnp.sum(second.astype(F32) * back4) + jnp.sum(own_g * (own_f + bias_second[:, 0:channels]))

    inside = (
        (row >= edge[0])
        & (row <= edge[1])
        & (column >= edge[2])
        & (column <= edge[3])
    )
    pulled = act_back(hidden, parts, gain_second, back, channels).reshape(shape4)
    hid[...] = jnp.where(inside, pulled, 0.0)
    back3[4:6] = jnp.zeros((2,) + back3.shape[1:], BF16)
    for dj in range(3):
        back3[0:4, :, :, LANES * dj : LANES * (dj + 1)] = hid[:, :, dj : dj + across, :].astype(BF16)

    def pack(which):
        lane = lax.broadcasted_iota(jnp.int32, (channels, LANES), 1)
        for group in range(7):
            if group == 6:
                last = jnp.full((channels, LANES), value, F32)
            else:
                last = taps[4 * group + 3]
            for k in range(3):
                tile = jnp.where(lane < channels, taps[4 * group + k], pltpu.roll(last, 96 - 32 * k, 1))
                for y in range(4):
                    for z in range(4):
                        packed[which, y, 42 * z + 6 * group : 42 * z + 6 * group + 6, LANES * k : LANES * (k + 1)] = tile[
                            24 * y + 6 * z : 24 * y + 6 * z + 6
                        ]

    turned = dot(perm[...], second.reshape(-1, LANES), ((1,), (1,))).astype(BF16)
    for pair in range(9):
        dt, di = divmod(pair, 3)
        got = dot(
            turned,
            map3[2 - dt : 2 - dt + frames, 3 - di : 3 - di + rows].reshape(-1, 3 * LANES),
            ((1,), (0,)),
        )
        for dj in range(3):
            taps[3 * pair + dj] = got[:, LANES * (2 - dj) : LANES * (3 - dj)]
    pack(1)

    first_own = first3[2 : 2 + frames, 2 : 2 + rows, 0:across, 2 * LANES : 3 * LANES].reshape(-1, LANES)
    turned = dot(perm[...], first_own, ((1,), (1,))).astype(BF16)
    low = jnp.zeros((frames * rows * across, LANES), F32)
    for pair in range(9):
        dt, di = divmod(pair, 3)
        moved = back3[2 - dt : 2 - dt + frames, 2 - di : 2 - di + rows].reshape(-1, 3 * LANES)
        low = low + dot(moved, w1b[pair], ((1,), (1,)))
        got = dot(turned, moved, ((1,), (0,)))
        for dj in range(3):
            taps[3 * pair + dj] = got[:, LANES * (2 - dj) : LANES * (3 - dj)]
    pack(0)

    gain_own = gain_first[:, 0:channels]
    parts = act_parts(own_f, gain_own, channels)
    low4 = low.reshape(frames, rows, across, LANES)[..., 0:channels]
    grad[...] = own_g + act_back(own_f, parts, gain_own, low4, channels)


def local_block(edge, ext, feats_own, map_own, k_first, k_second, vectors, perm):
    frames, rows, across, channels = feats_own.shape
    vmem = pl.BlockSpec(memory_space=pltpu.VMEM)
    return pl.pallas_call(
        block_kernel,
        out_shape=(
            jax.ShapeDtypeStruct(feats_own.shape, F32),
            jax.ShapeDtypeStruct((2, 4, 168, 3 * LANES), F32),
        ),
        in_specs=[pl.BlockSpec(memory_space=pltpu.SMEM)] + [vmem] * 7,
        out_specs=(vmem, vmem),
        scratch_shapes=[
            pltpu.VMEM((frames, rows + 4, PITCH + 8, LANES), F32),
            pltpu.VMEM((frames + 2, rows + 4, PITCH, 3 * LANES), BF16),
            pltpu.VMEM((frames + 2, rows + 4, PITCH, 3 * LANES), BF16),
            pltpu.VMEM((frames, rows + 2, PITCH, LANES), F32),
            pltpu.VMEM((frames + 2, rows + 2, across, 3 * LANES), BF16),
            pltpu.VMEM((9, 3 * LANES, LANES), BF16),
            pltpu.VMEM((9, LANES, 3 * LANES), BF16),
            pltpu.VMEM((9, LANES, 3 * LANES), BF16),
            pltpu.VMEM((27, channels, LANES), F32),
        ],
        compiler_params=pltpu.CompilerParams(vmem_limit_bytes=48 * 1024 * 1024),
        cost_estimate=pl.CostEstimate(flops=3_000_000_000, bytes_accessed=6_000_000, transcendentals=500_000),
    )(edge, ext, feats_own, map_own, k_first, k_second, vectors, perm)


def extended(cells, axis, dim, width):
    count = lax.axis_size(axis)
    ends = count - 1
    head = lax.slice_in_dim(cells, 0, width, axis=dim)
    tail = lax.slice_in_dim(cells, cells.shape[dim] - width, cells.shape[dim], axis=dim)
    return jnp.concatenate(
        [
            lax.ppermute(tail, axis, [(i, (i + 1) % count) for i in range(ends)]),
            cells,
            lax.ppermute(head, axis, [((i + 1) % count, i) for i in range(ends)]),
        ],
        axis=dim,
    )


def swap(values, axis, flip):
    return lax.ppermute(values, axis, [(i, i ^ flip) for i in range(lax.axis_size(axis))])


def pick(values, index):
    return lax.dynamic_index_in_dim(values, index, 0, keepdims=False)


def local(
    features,
    gain_first,
    bias_first,
    kernel_first,
    gain_second,
    bias_second,
    kernel_second,
    reward_map,
    target_scores,
):
    frames, rows, across, channels = features.shape[1:]
    count_h = lax.axis_size("ha")
    count_w = lax.axis_size("wa")
    at_h = lax.axis_index("ha")
    at_w = lax.axis_index("wa")
    at_col = lax.axis_index("col")
    core = at_w % 2
    at_y = at_h % 4
    at_z = at_h // 4

    both = jnp.concatenate([features[0], reward_map[0]], 0)
    ext = extended(extended(both, "ha", 1, 2), "wa", 2, 2)
    edge = jnp.stack(
        [
            jnp.where(at_h == 0, 1, 0),
            jnp.where(at_h == count_h - 1, rows, rows + 1),
            jnp.where(at_w == 0, 1, 0),
            jnp.where(at_w == count_w - 1, across, across + 1),
        ]
    ).astype(jnp.int32)
    vectors = jnp.pad(
        jnp.stack([gain_first, bias_first, gain_second, bias_second]), ((0, 4), (0, LANES - channels))
    )
    place = lax.broadcasted_iota(jnp.int32, (channels, LANES), 0)
    source = 24 * ((place // 6) % 4) + 6 * (place // 24) + place % 6
    perm = (lax.broadcasted_iota(jnp.int32, (channels, LANES), 1) == source).astype(BF16)
    grad, packed = local_block(
        edge,
        ext,
        features[0],
        reward_map[0],
        kernel_first.reshape(27, channels, channels),
        kernel_second.reshape(27, channels, channels),
        vectors,
        perm,
    )

    held = pick(packed, core) + swap(pick(packed, 1 - core), "wa", 1)
    got = [swap(pick(held, at_y ^ k), "ha", k) for k in (1, 2, 3)]
    held = (pick(held, at_y) + got[0]) + (got[1] + got[2])
    held = held.reshape(4, 42, 3 * LANES)
    got = [swap(pick(held, at_z ^ k), "ha", 4 * k) for k in (1, 2, 3)]
    held = (pick(held, at_z) + got[0]) + (got[1] + got[2])
    got = [swap(held, "wa", 2 * k) for k in (1, 2, 3)]
    held = (held + got[0]) + (got[1] + got[2])
    other = swap(held, "col", 1)
    each = [jnp.where(at_col == 0, held, other), jnp.where(at_col == 0, other, held)]
    total = count_h * count_w * rows * across * frames
    norm_reward = jnp.sqrt(jnp.float32(total * channels))
    rewards = [part[36, 96] / norm_reward for part in each]
    deltas = []
    for n in range(2):
        prob = 1.0 / (1.0 + jnp.exp(rewards[1 - n] - rewards[n]))
        target = 1.0 / (1.0 + jnp.exp(target_scores[1 - n] - target_scores[n]))
        deltas.append(prob - target)
    summed = (each[0] * deltas[0] + each[1] * deltas[1]) * (1.0 / jnp.sqrt(jnp.float32(total)))
    mate = swap(summed, "wa", 1)
    pair = jnp.stack([jnp.where(core == 0, summed, mate), jnp.where(core == 0, mate, summed)])
    pair = pair.reshape(2, 7, 6, 3, LANES)
    main = jnp.moveaxis(pair[..., 0:channels], 3, 2)
    rest = pair[..., channels:LANES].reshape(2, 7, 6, 1, channels)
    rest = jnp.moveaxis(rest, 3, 2)
    weights = jnp.concatenate([main, rest], axis=2).reshape(2, 28, 6, channels)[:, 0:27]
    mine = jnp.where(at_col == 0, deltas[0], deltas[1])
    return ((grad * mine)[None], weights.reshape(2, 3, 3, 3, 6, channels))


def solution(mesh):
    placed = (
        P("col", None, "ha", "wa", None),
        P(),
        P(),
        P(),
        P(),
        P(),
        P(),
        P("col", None, "ha", "wa", None),
        P(),
    )
    return jax.shard_map(
        local,
        mesh=mesh,
        in_specs=placed,
        out_specs=(P("col", None, "ha", "wa", None), P(None, None, None, None, "ha", None)),
        check_vma=False,
    )
```
